256 devices in a mesh: rep: 32 (over y, z_hi, x), fsdp: 8 (over z_lo, core).
Axes of the slice: x: 4, y: 4, z: 8 (z_hi: 2, z_lo: 4; z = z_hi * 4 + z_lo), core: 2. Of those that a mesh axis runs over, the one named last changes fastest.
Arguments:
- inputs: bfloat16 [2, 32, 2048, 4096], P(None, 'rep', 'fsdp'), may hold values from -6 to 6
- targets: bfloat16 [2, 32, 2048, 512], P(None, 'rep', 'fsdp'), may hold values from -6 to 6
- weights: bfloat16 [32, 4096, 512], P('rep', 'fsdp'), may hold values from -6 to 6
- first_moment: float32 [32, 4096, 512], P('rep', 'fsdp'), may hold values from -0.0078125 to 0.0078125
- second_moment: float32 [32, 4096, 512], P('rep', 'fsdp'), may hold values from 2.5e-08 to 1e-06
- global_weights: float32 [4096, 512], P('fsdp'), may hold values from -6 to 6
- outer_moment: float32 [4096, 512], P('fsdp'), may hold values from -4 to 4
- drift: float32 [32, 4096, 512], P('rep', 'fsdp'), may hold values from -6 to 6
Outputs:
- weights_out: bfloat16 [32, 4096, 512], P('rep', 'fsdp')
- global_out: float32 [4096, 512], P('fsdp')
The draws below stay inside these ranges and needn't reach their ends.
All inputs are finite; a program needn't handle non-finite values.
Results may differ from the reference program's by a relative error of at most 0.0065.
Values may be sent and summed in bfloat16 or wider, within the bound.
No kernel may reach another device: no remote copies, remote signals or barrier semaphores. Data moves between devices by JAX's collectives and lax.ppermute only.
A program may use at most 128 MiB of HBM per device.

```python
import math
import jax
import jax.numpy as jnp
from jax import lax

D = 4096
KV = 512
STEPS = 2
TOKENS = 2048
REPLICAS = 32


def levels(stream_key, dims, shards, least, largest):
    loudness, own = 1.0, jax.random.fold_in(stream_key, 6)
    for axis_at, blocks in shards:
        steps = jnp.exp(jax.random.uniform(jax.random.fold_in(own, axis_at), (blocks,), jnp.float32, least / len(shards), largest / len(shards)))
        loudness = loudness * jnp.repeat(steps, dims[axis_at] // blocks).reshape([-1 if axis == axis_at else 1 for axis in range(len(dims))])
    return loudness


def gaussian(key, shape, deviation, reach, split=(), kind=jnp.bfloat16):
    array = jax.random.normal(key, shape, jnp.float32) * deviation
    if len(split) > 0:
        array = levels(key, shape, split, -0.22, 0.18) * array
    return jnp.clip(array, min=-reach, max=reach).astype(kind)


def setup_inputs(seed: int = 0) -> dict:
    key_list = jax.random.split(jax.random.key(seed), 9)
    inputs = gaussian(key_list[0], (STEPS, REPLICAS, TOKENS, D), 1.0, 6.0, ((1, 32), (2, 8)))
    targets = gaussian(key_list[1], (STEPS, REPLICAS, TOKENS, KV), 1.0, 6.0, ((1, 32), (2, 8)))
    weights = gaussian(key_list[2], (REPLICAS, D, KV), 1.0, 6.0, ((0, 32), (1, 8)))
    first_moment = gaussian(key_list[3], (REPLICAS, D, KV), 0.0005, 0.0078125, ((0, 32), (1, 8)), jnp.float32)
    second_moment = jnp.clip(jnp.exp(math.log(9.999999974752427e-07) - 3.6888794 * jax.random.uniform(key_list[4], (REPLICAS, D, KV), jnp.float32) ** levels(key_list[4], (REPLICAS, D, KV), ((0, 32), (1, 8)), -0.2, 0.2)), 2.5000000292152436e-08, 9.999999974752427e-07)
    global_weights = gaussian(key_list[5], (D, KV), 1.0, 6.0, ((0, 8),), jnp.float32)
    outer_moment = gaussian(key_list[6], (D, KV), 0.3, 4.0, ((0, 8),), jnp.float32)
    drift = gaussian(key_list[7], (REPLICAS, D, KV), 0.5, 6.0, ((0, 32), (1, 8)), jnp.float32)
    return dict(inputs=inputs, targets=targets, weights=weights, first_moment=first_moment, second_moment=second_moment, global_weights=global_weights, outer_moment=outer_moment, drift=drift)


inner_rate = 0.2
beta_first = 0.9
beta_second = 0.95
adam_eps = 1e-08
decay_rate = 0.1
mix_share = 0.5
outer_rate = 0.7
outer_beta = 0.9

def reference(inputs, targets, weights, first_moment, second_moment, global_weights, outer_moment, drift):
    mean_drift = lax.optimization_barrier(jnp.sum(drift, axis=0)) / REPLICAS
    new_moment = outer_beta * outer_moment + mean_drift
    global_out = global_weights - outer_rate * (mean_drift + outer_beta * new_moment)
    scale = D ** (-0.5)

    def replica(index):
        current = weights[index]
        moment_one = first_moment[index]
        moment_two = second_moment[index]
        for step in range(STEPS):
            feats = inputs[step, index]
            keys = jnp.dot(feats, current, preferred_element_type=jnp.float32) * scale
            residual = (keys - targets[step, index].astype(jnp.float32)).astype(jnp.bfloat16)
            grad = jnp.dot(feats.T, residual, preferred_element_type=jnp.float32) * (scale / TOKENS)
            moment_one = beta_first * moment_one + (1.0 - beta_first) * grad
            moment_two = beta_second * moment_two + (1.0 - beta_second) * grad * grad
            wide = current.astype(jnp.float32)
            updated = wide - inner_rate * (moment_one / (jnp.sqrt(moment_two) + adam_eps) + decay_rate * wide)
            if step == 0:
                updated = mix_share * updated + (1.0 - mix_share) * global_out
            current = updated.astype(jnp.bfloat16)
        return current
    weights_out = lax.map(replica, jnp.arange(REPLICAS, dtype=jnp.int32))
    return (weights_out, global_out)
```

```python
import jax
import jax.numpy as jnp
from jax import lax
from jax.sharding import PartitionSpec as P

STEPS = 2
CHUNKS = 2

inner_rate = 0.2
beta_first = 0.9
beta_second = 0.95
adam_eps = 1e-08
decay_rate = 0.1
mix_share = 0.5
outer_rate = 0.7
outer_beta = 0.9

BF = jnp.bfloat16
F32 = jnp.float32


def xor_perm(size, stride, extent, k):
    pairs = []
    for i in range(size):
        at = (i // stride) % extent
        pairs.append((i, i + ((at ^ k) - at) * stride))
    return pairs


def swap(value, axis, stride, extent, k):
    return lax.ppermute(value, axis, xor_perm(lax.axis_size(axis), stride, extent, k))


def core_swap(value):
    return swap(value, "fsdp", 1, 2, 1)


def z_swap(value, k):
    return swap(value, "fsdp", 2, 4, k)


def scatter_sum(value, me, stride, extent):
    rows = value.shape[0] // extent
    total = lax.dynamic_slice_in_dim(value, me * rows, rows).astype(F32)
    for k in range(1, extent):
        piece = lax.dynamic_slice_in_dim(value, (me ^ k) * rows, rows)
        total = total + swap(piece, "rep", stride, extent, k).astype(F32)
    return total


def gather(value, me, stride, extent):
    rows = value.shape[0]
    whole = jnp.zeros((rows * extent,) + value.shape[1:], value.dtype)
    whole = lax.dynamic_update_slice_in_dim(whole, value, me * rows, 0)
    for k in range(1, extent):
        piece = swap(value, "rep", stride, extent, k)
        whole = lax.dynamic_update_slice_in_dim(whole, piece, (me ^ k) * rows, 0)
    return whole


def mean_of_drift(drift):
    at = lax.axis_index("rep")
    replicas = lax.axis_size("rep")
    x, z_hi, y = at % 4, (at // 4) % 2, at // 8
    part = drift.astype(BF)
    part = scatter_sum(part, x, 1, 4).astype(BF)
    part = scatter_sum(part, y, 8, 4).astype(BF)
    part = scatter_sum(part, z_hi, 4, 2)
    part = (part / replicas).astype(BF)
    part = gather(part, z_hi, 4, 2)
    part = gather(part, y, 8, 4)
    return gather(part, x, 1, 4).astype(F32)


def outer_update(global_weights, outer_moment, drift):
    mean_drift = mean_of_drift(drift)
    new_moment = outer_beta * outer_moment + mean_drift
    return global_weights - outer_rate * (mean_drift + outer_beta * new_moment)


def per_device(
    inputs, targets, weights, first_moment, second_moment, global_weights, outer_moment, drift
):
    at = lax.axis_index("fsdp")
    core, z = at % 2, at // 2
    tok_rows, width = inputs.shape[2], inputs.shape[3]
    tokens_total = tok_rows * lax.axis_size("fsdp")
    scale = width ** (-0.5)
    rows, columns = weights.shape[1], weights.shape[2]
    cols = columns // CHUNKS

    def half(feats, parity):
        return jnp.concatenate(
            [
                lax.dynamic_slice_in_dim(feats, (2 * (z ^ j) + parity) * rows, rows, 1)
                for j in range(4)
            ],
            axis=1,
        )

    feats, aims = [], []
    for step in range(STEPS):
        mine = half(inputs[step, 0], core)
        theirs = core_swap(half(inputs[step, 0], 1 - core))
        feats.append(jnp.concatenate([mine, theirs], axis=0))
        aim = targets[step, 0]
        aims.append(jnp.concatenate([aim, core_swap(aim)], axis=0))

    global_out = outer_update(global_weights, outer_moment, drift[0])

    current = [weights[0][:, k * cols : (k + 1) * cols] for k in range(CHUNKS)]
    ones = [first_moment[0][:, k * cols : (k + 1) * cols] for k in range(CHUNKS)]
    twos = [second_moment[0][:, k * cols : (k + 1) * cols] for k in range(CHUNKS)]
    for step in range(STEPS):
        for k in range(CHUNKS):
            own = current[k]
            near = z_swap(own, 1)
            far = z_swap(own, 3)
            rest = z_swap(far, 1)
            whole = jnp.concatenate([own, near, rest, far], axis=0)
            part = jnp.dot(feats[step], whole, preferred_element_type=F32)
            other = core_swap(part)
            other = jnp.concatenate([other[tok_rows:], other[:tok_rows]], axis=0)
            aim = aims[step][:, k * cols : (k + 1) * cols].astype(F32)
            residual = ((part + other) * scale - aim).astype(BF)
            grads = lax.dot_general(
                feats[step], residual, (((0,), (0,)), ((), ())), preferred_element_type=F32
            ).reshape(4, rows, cols)
            passed = z_swap(grads[2].astype(BF), 1)
            from_near = z_swap(grads[1].astype(BF), 1)
            from_far = z_swap((grads[3] + passed.astype(F32)).astype(BF), 3)
            grad = (grads[0] + from_near.astype(F32) + from_far.astype(F32)) * (
                scale / tokens_total
            )
            ones[k] = beta_first * ones[k] + (1.0 - beta_first) * grad
            twos[k] = beta_second * twos[k] + (1.0 - beta_second) * grad * grad
            wide = own.astype(F32)
            updated = wide - inner_rate * (
                ones[k] / (jnp.sqrt(twos[k]) + adam_eps) + decay_rate * wide
            )
            if step == 0:
                outer = global_out[:, k * cols : (k + 1) * cols]
                updated = mix_share * updated + (1.0 - mix_share) * outer
            current[k] = updated.astype(BF)
    return (jnp.concatenate(current, axis=1)[None], global_out)


def solution(mesh):
    in_specs = (
        P(None, "rep", "fsdp", None),
        P(None, "rep", "fsdp", None),
        P("rep", "fsdp", None),
        P("rep", "fsdp", None),
        P("rep", "fsdp", None),
        P("fsdp", None),
        P("fsdp", None),
        P("rep", "fsdp", None),
    )
    out_specs = (P("rep", "fsdp", None), P("fsdp", None))
    return jax.shard_map(
        per_device, mesh=mesh, in_specs=in_specs, out_specs=out_specs, check_vma=False
    )
```

```python
import functools

import jax
import jax.numpy as jnp
from jax import lax
from jax.experimental import pallas as pl
from jax.experimental.pallas import tpu as pltpu
from jax.sharding import PartitionSpec as P

CHUNKS = 2

inner_rate = 0.2
beta_first = 0.9
beta_second = 0.95
adam_eps = 1e-08
decay_rate = 0.1
mix_share = 0.5
outer_rate = 0.7
outer_beta = 0.9

BF = jnp.bfloat16
F32 = jnp.float32
VMEM_LIMIT = 16 << 20
PREPARE_LIMIT = 56 << 20
FLOPS = 10**11

ANY = pl.BlockSpec(memory_space=pl.ANY)
FULL = pl.BlockSpec(memory_space=pltpu.VMEM)
SCALAR = pl.BlockSpec(memory_space=pltpu.SMEM)


def swap(value, axis, change):
    pairs = [(i, change(i)) for i in range(lax.axis_size(axis))]
    return lax.ppermute(value, axis, pairs)


def pair_swap(value, g):
    return swap(value, "fsdp", lambda i: i ^ g)


def far_swap(value):
    return swap(value, "fsdp", lambda i: i ^ 6)


def shaped(shape, dtype):
    return jax.ShapeDtypeStruct(shape, dtype)


def call(body, outs, operands, gates=(), specs=None, limit=VMEM_LIMIT, scratch=()):
    n = len(gates)
    size = sum(v.size * v.dtype.itemsize for v in operands)

    def kernel(*refs):
        body(*refs[n:])

    return pl.pallas_call(
        kernel,
        name=getattr(body, "func", body).__name__.removesuffix("_kernel"),
        grid=(1,),
        out_shape=outs,
        in_specs=[ANY] * n + (specs or [FULL] * len(operands)),
        out_specs=jax.tree.map(lambda _: FULL, outs),
        scratch_shapes=scratch,
        compiler_params=pltpu.CompilerParams(vmem_limit_bytes=limit),
        cost_estimate=pl.CostEstimate(flops=FLOPS, bytes_accessed=size, transcendentals=0),
    )(*gates, *operands)


def prepare_kernel(step, groups, depth, place, feats, *refs):
    outs, done = refs[:-1], refs[-1]
    copies = []
    for g, out in zip(groups, outs):
        at = place[0] ^ g
        for j, shard in enumerate((at, at ^ 6)):
            columns = pl.ds(pl.multiple_of(shard * depth, depth), depth)
            copies.append(
                pltpu.make_async_copy(
                    feats.at[step, 0, :, columns],
                    out.at[:, j * depth : (j + 1) * depth],
                    done.at[len(copies)],
                )
            )
    for copy in copies:
        copy.start()
    for copy in copies:
        copy.wait()


def keys_kernel(scale, place, *refs):
    feats, chunks, (kept, sent, whole) = refs[:4], refs[4:-3], refs[-3:]
    rows = feats[0].shape[0]
    core = place[0] % 2
    for k in range(len(chunks) // 3):
        aims, own, far = chunks[3 * k : 3 * k + 3]
        depth, cols = own.shape[0], own.shape[1] // 2
        for g in range(4):
            part = jnp.dot(feats[g][:, :depth], own[...], preferred_element_type=F32)
            part += jnp.dot(feats[g][:, depth:], far[...], preferred_element_type=F32)
            part *= scale
            if g == 0:
                part -= aims[...].astype(F32)
            whole[...] = part
            for half, out in ((1 - core, sent), (core, kept)):
                columns = pl.ds(pl.multiple_of(half * cols, cols), cols)
                out[g * rows : (g + 1) * rows, k * cols : (k + 1) * cols] = whole[:, columns]


def core_sum_kernel(*refs):
    pairs, out = refs[:-1], refs[-1]
    rows = out.shape[0] // 4
    cols = pairs[0].shape[1]
    for k in range(len(pairs) // 2):
        kept, other = pairs[2 * k : 2 * k + 2]
        for g in range(4):
            here, there = g * rows, (g ^ 1) * rows
            total = kept[here : here + rows] + other[there : there + rows]
            out[here : here + rows, k * cols : (k + 1) * cols] = total.astype(BF)


def residual_kernel(part, other, out):
    rows = out.shape[0] // 4
    for g in range(4):
        here, there = g * rows, (g ^ 2) * rows
        total = part[here : here + rows].astype(F32) + other[there : there + rows].astype(F32)
        out[here : here + rows] = total.astype(BF)


def grads_kernel(shard, place, *refs):
    feats, (mine, other), outs, whole = refs[:4], refs[4:6], refs[6:-1], refs[-1]
    rows, depth = feats[0].shape[0], outs[0].shape[0]
    core = place[0] % 2
    cols = mine.shape[1] // CHUNKS
    for k in range(CHUNKS):
        part = slice(k * cols, (k + 1) * cols)
        for half, residual, flip in ((core, mine, 0), (1 - core, other, 1)):
            columns = pl.ds(pl.multiple_of((2 * k + half) * cols, cols), cols)
            for g in range(4):
                there = (g ^ flip) * rows
                whole[g * rows : (g + 1) * rows, columns] = residual[there : there + rows, part]
    at = slice(shard * depth, (shard + 1) * depth)
    dims = (((0,), (0,)), ((), ()))
    total = None
    for g in range(4):
        term = lax.dot_general(
            feats[g][:, at],
            whole[g * rows : (g + 1) * rows],
            dims,
            preferred_element_type=F32,
        )
        total = term if total is None else total + term
    cols = outs[0].shape[1]
    for k, out in enumerate(outs):
        out[...] = total[:, k * cols : (k + 1) * cols].astype(out.dtype)


def cast_kernel(drift, out):
    share, rows = out.shape[0], out.shape[1]
    for i in range(share):
        out[i] = drift[0, i * rows : (i + 1) * rows].astype(BF)


def sum_kernel(pieces, out):
    out[...] = jnp.sum(pieces[...].astype(F32), axis=0).astype(BF)


def mean_kernel(replicas, part, other, out):
    mean = ((part[...].astype(F32) + other[...].astype(F32)) / replicas).astype(BF)
    out[...] = jnp.broadcast_to(mean[None], out.shape)


def planes(size):
    return [[i for i in range(size) if (i // 4) % 2 == hi] for hi in range(2)]


def adam(factor, kept, far, own, one, two):
    grad = (kept + far.astype(F32)) * factor
    one = beta_first * one + (1.0 - beta_first) * grad
    two = beta_second * two + (1.0 - beta_second) * grad * grad
    wide = own.astype(F32)
    updated = wide - inner_rate * (one / (jnp.sqrt(two) + adam_eps) + decay_rate * wide)
    return one, two, updated


def first_update_kernel(factor, kept, far, own, one, two, outer, new, new_one, new_two):
    first, second, updated = adam(factor, kept[...], far[...], own[...], one[...], two[...])
    new_one[...] = first
    new_two[...] = second
    new[...] = (mix_share * updated + (1.0 - mix_share) * outer[...]).astype(BF)


def update_kernel(factor, kept, far, own, one, two, *rest):
    done, out = rest[:-1], rest[-1]
    _, _, updated = adam(factor, kept[...], far[...], own[...], one[...], two[...])
    cols = updated.shape[1]
    if done:
        for k, block in enumerate(done):
            out[0, :, k * cols : (k + 1) * cols] = block[...]
        out[0, :, len(done) * cols :] = updated.astype(BF)
    else:
        out[...] = updated.astype(BF)


def outer_kernel(pieces, global_weights, outer_moment, out):
    share, rows = pieces.shape[0], pieces.shape[1]
    for i in range(share):
        at = slice(i * rows, (i + 1) * rows)
        mean_drift = pieces[i].astype(F32)
        new_moment = outer_beta * outer_moment[at] + mean_drift
        out[at] = global_weights[at] - outer_rate * (mean_drift + outer_beta * new_moment)


def per_device(
    inputs, targets, weights, first_moment, second_moment, global_weights, outer_moment, drift
):
    place = lax.axis_index("fsdp").astype(jnp.int32).reshape(1)
    tok_rows, width = inputs.shape[2], inputs.shape[3]
    tokens_total = tok_rows * lax.axis_size("fsdp")
    scale = width ** (-0.5)
    rows, columns = weights.shape[1], weights.shape[2]
    wide = columns // CHUNKS
    cols = wide // 2
    factor = scale / tokens_total
    replicas = lax.axis_size("rep")
    groups = planes(replicas)
    share = len(groups[0])

    def prepare(step, wanted, gates):
        return call(
            functools.partial(prepare_kernel, step, wanted, rows),
            [shaped((tok_rows, 2 * rows), BF)] * len(wanted),
            [place, inputs],
            gates,
            [SCALAR, ANY],
            limit=PREPARE_LIMIT,
            scratch=[pltpu.SemaphoreType.DMA((2 * len(wanted),))],
        )

    def chunk(lead, k):
        at = lead + (0, k)
        height = tok_rows if len(lead) > 1 else rows
        return pl.BlockSpec((None,) * len(lead) + (height, wide), lambda i: at)

    def keys(step, feats, chunks, own, far, gates):
        views, specs = [], []
        for k in chunks:
            views += [targets, own, far]
            specs += [chunk((step, 0), k)] + ([chunk((0,), k)] if step == 0 else [FULL]) * 2
        return call(
            functools.partial(keys_kernel, scale),
            [shaped((4 * tok_rows, len(chunks) * cols), F32)] * 2,
            [place, *feats, *views],
            gates,
            [SCALAR] + [FULL] * 4 + specs,
            scratch=[pltpu.VMEM((tok_rows, wide), F32)],
        )

    def core_sum(pairs, gates):
        blocks = []
        for kept, sent in pairs:
            blocks += [kept, pair_swap(sent, 1)]
        out = shaped((4 * tok_rows, columns // 2), BF)
        return call(core_sum_kernel, out, blocks, gates)

    def residuals(part, gates):
        return call(residual_kernel, shaped(part.shape, BF), [part, pair_swap(part, 2)], gates)

    def grads(shard, dtype, parts, feats, mine, other, gates):
        return call(
            functools.partial(grads_kernel, shard),
            [shaped((rows, columns // parts), dtype)] * parts,
            [place, *feats, mine, other],
            gates,
            [SCALAR] + [FULL] * 6,
            scratch=[pltpu.VMEM((4 * tok_rows, columns), BF)],
        )

    def first_update(k, kept, far, gates):
        state = chunk((0,), k)
        block = shaped((rows, wide), F32)
        return call(
            functools.partial(first_update_kernel, factor),
            [shaped((rows, wide), BF), block, block],
            [kept, far, weights, first_moment, second_moment, global_out],
            gates,
            [chunk((), k), FULL, state, state, state, chunk((), k)],
        )

    def update(k, kept, far, own, one, two, done, gates):
        return call(
            functools.partial(update_kernel, factor),
            shaped((1, rows, columns) if done else (rows, wide), BF),
            [kept, far, own, one, two, *done],
            gates,
            [chunk((), k)] + [FULL] * (4 + len(done)),
        )

    far = far_swap(weights)
    packs = prepare(0, (0, 1, 2, 3), [])
    feats = [packs[0]] + [pair_swap(packs[g], g) for g in (1, 2, 3)]
    rows_of = rows // share
    casted = call(cast_kernel, shaped((share, rows_of, columns), BF), [drift], [feats[1]])
    pieces = lax.all_to_all(casted, "rep", 0, 0, axis_index_groups=groups)
    packs = prepare(1, (0, 1, 2, 3), [casted])
    summed = call(sum_kernel, shaped((rows_of, columns), BF), [pieces], [packs[0]])
    summed_other = swap(summed, "rep", lambda i: i ^ 4)

    both = keys(0, feats, (0, 1), weights, far, [summed])
    part = core_sum([both], [])
    copies = call(
        functools.partial(mean_kernel, replicas),
        shaped((share, rows_of, columns), BF),
        [summed, summed_other],
        [part],
    )
    means = lax.all_to_all(copies, "rep", 0, 0, axis_index_groups=groups)
    mine = residuals(part, [means])
    other = pair_swap(mine, 1)
    across_a, across_b = grads(1, BF, CHUNKS, feats, mine, other, [])
    far_a, far_b = far_swap(across_a), far_swap(across_b)
    later = [packs[0]] + [pair_swap(packs[g], g) for g in (1, 2, 3)]
    (kept,) = grads(0, F32, 1, feats, mine, other, [across_b])
    global_out = call(
        outer_kernel,
        shaped((rows, columns), F32),
        [means, global_weights, outer_moment],
        [kept],
    )
    own_a, one_a, two_a = first_update(0, kept, far_a, [])
    gather_a = far_swap(own_a)
    own_b, one_b, two_b = first_update(1, kept, far_b, [own_a, *later[1:3]])
    gather_b = far_swap(own_b)

    keys_a = keys(1, later, (0,), own_a, gather_a, [own_b])
    keys_b = keys(1, later, (1,), own_b, gather_b, [keys_a[0]])
    part = core_sum([keys_a, keys_b], [])
    mine = residuals(part, [])
    other = pair_swap(mine, 1)
    across_a, across_b = grads(1, BF, CHUNKS, later, mine, other, [])
    far_a, far_b = far_swap(across_a), far_swap(across_b)
    (kept,) = grads(0, F32, 1, later, mine, other, [across_b])
    done_a = update(0, kept, far_a, own_a, one_a, two_a, [], [])
    weights_out = update(1, kept, far_b, own_b, one_b, two_b, [done_a], [])
    return (weights_out, global_out)


def solution(mesh):
    in_specs = (
        P(None, "rep", "fsdp", None),
        P(None, "rep", "fsdp", None),
        P("rep", "fsdp", None),
        P("rep", "fsdp", None),
        P("rep", "fsdp", None),
        P("fsdp", None),
        P("fsdp", None),
        P("rep", "fsdp", None),
    )
    out_specs = (P("rep", "fsdp", None), P("fsdp", None))
    return jax.shard_map(
        per_device, mesh=mesh, in_specs=in_specs, out_specs=out_specs, check_vma=False
    )
```

```python
import functools

import jax
import jax.numpy as jnp
from jax import lax
from jax.experimental import pallas as pl
from jax.experimental.pallas import tpu as pltpu
from jax.sharding import PartitionSpec as P

CHUNKS = 2

inner_rate = 0.2
beta_first = 0.9
beta_second = 0.95
adam_eps = 1e-08
decay_rate = 0.1
mix_share = 0.5
outer_rate = 0.7
outer_beta = 0.9

BF = jnp.bfloat16
F32 = jnp.float32
VMEM_LIMIT = 16 << 20
PREPARE_LIMIT = 56 << 20
FLOPS = 10**11

ANY = pl.BlockSpec(memory_space=pl.ANY)
FULL = pl.BlockSpec(memory_space=pltpu.VMEM)
SCALAR = pl.BlockSpec(memory_space=pltpu.SMEM)


def swap(value, axis, change):
    pairs = [(i, change(i)) for i in range(lax.axis_size(axis))]
    return lax.ppermute(value, axis, pairs)


def pair_swap(value, g):
    return swap(value, "fsdp", lambda i: i ^ g)


def far_swap(value):
    return swap(value, "fsdp", lambda i: i ^ 6)


def shaped(shape, dtype):
    return jax.ShapeDtypeStruct(shape, dtype)


def call(body, outs, operands, gates=(), specs=None, limit=VMEM_LIMIT, scratch=()):
    n = len(gates)
    size = sum(v.size * v.dtype.itemsize for v in operands)

    def kernel(*refs):
        body(*refs[n:])

    return pl.pallas_call(
        kernel,
        name=getattr(body, "func", body).__name__.removesuffix("_kernel"),
        grid=(1,),
        out_shape=outs,
        in_specs=[ANY] * n + (specs or [FULL] * len(operands)),
        out_specs=jax.tree.map(lambda _: FULL, outs),
        scratch_shapes=scratch,
        compiler_params=pltpu.CompilerParams(vmem_limit_bytes=limit),
        cost_estimate=pl.CostEstimate(flops=FLOPS, bytes_accessed=size, transcendentals=0),
    )(*gates, *operands)


def prepare_kernel(step, groups, depth, place, feats, *refs):
    outs, done = refs[:-1], refs[-1]
    copies = []
    for g, out in zip(groups, outs):
        at = place[0] ^ g
        for j, shard in enumerate((at, at ^ 6)):
            columns = pl.ds(pl.multiple_of(shard * depth, depth), depth)
            copies.append(
                pltpu.make_async_copy(
                    feats.at[step, 0, :, columns],
                    out.at[:, j * depth : (j + 1) * depth],
                    done.at[len(copies)],
                )
            )
    for copy in copies:
        copy.start()
    for copy in copies:
        copy.wait()


def keys_kernel(scale, count, own_first, place, *refs):
    feats, chunks, (kept, sent, whole) = refs[:count], refs[count:-3], refs[-3:]
    rows = feats[0].shape[0]
    core = place[0] % 2
    for k in range(len(chunks) // 3):
        aims, own, far = chunks[3 * k : 3 * k + 3]
        depth, cols = own.shape[0], own.shape[1] // 2
        for g in range(count):
            part = jnp.dot(feats[g][:, :depth], own[...], preferred_element_type=F32)
            part += jnp.dot(feats[g][:, depth:], far[...], preferred_element_type=F32)
            part *= scale
            if g == 0 and own_first:
                part -= aims[...].astype(F32)
            whole[...] = part
            for half, out in ((1 - core, sent), (core, kept)):
                columns = pl.ds(pl.multiple_of(half * cols, cols), cols)
                out[g * rows : (g + 1) * rows, k * cols : (k + 1) * cols] = whole[:, columns]


def core_sum_kernel(rows, *refs):
    pairs, out = refs[:-1], refs[-1]
    cols = pairs[0].shape[1]
    for k in range(len(pairs) // 2):
        kept, other = pairs[2 * k : 2 * k + 2]
        for g in range(out.shape[0] // rows):
            here, there = g * rows, (g ^ 1) * rows
            total = kept[here : here + rows] + other[there : there + rows]
            out[here : here + rows, k * cols : (k + 1) * cols] = total.astype(BF)


def turn_kernel(*refs):
    feats, outs = refs[:4], refs[4:]
    rows, depth = feats[0].shape[0], outs[0].shape[0]
    for j, out in enumerate(outs):
        for g in range(4):
            out[:, g * rows : (g + 1) * rows] = feats[g][:, j * depth : (j + 1) * depth].T


def residual_kernel(*refs):
    ours, theirs, out = refs[: len(refs) // 2], refs[len(refs) // 2 : -1], refs[-1]
    half = out.shape[0] // 2
    if len(ours) == 1:
        ours = (ours[0].at[:half], ours[0].at[half:])
        theirs = (theirs[0].at[:half], theirs[0].at[half:])
    for i in range(2):
        total = ours[i][...].astype(F32) + theirs[1 - i][...].astype(F32)
        out[i * half : (i + 1) * half] = total.astype(BF)


def grads_kernel(place, feats, mine, other, *refs):
    outs, whole = refs[:-1], refs[-1]
    rows = mine.shape[0] // 4
    core = place[0] % 2
    cols = mine.shape[1] // CHUNKS
    for k in range(CHUNKS):
        part = slice(k * cols, (k + 1) * cols)
        for half, residual, flip in ((core, mine, 0), (1 - core, other, 1)):
            columns = pl.ds(pl.multiple_of((2 * k + half) * cols, cols), cols)
            for g in range(4):
                there = (g ^ flip) * rows
                whole[g * rows : (g + 1) * rows, columns] = residual[there : there + rows, part]
    cols = outs[0].shape[1]
    for k, out in enumerate(outs):
        part = whole[:, k * cols : (k + 1) * cols]
        grad = jnp.dot(feats[...], part, preferred_element_type=F32)
        out[...] = grad.astype(out.dtype)


def cast_kernel(drift, out):
    share, rows = out.shape[0], out.shape[1]
    for i in range(share):
        out[i] = drift[0, i * rows : (i + 1) * rows].astype(BF)


def sum_kernel(pieces, out):
    out[...] = jnp.sum(pieces[...].astype(F32), axis=0).astype(BF)


def mean_kernel(replicas, part, other, out):
    mean = ((part[...].astype(F32) + other[...].astype(F32)) / replicas).astype(BF)
    out[...] = jnp.broadcast_to(mean[None], out.shape)


def planes(size):
    return [[i for i in range(size) if (i // 4) % 2 == hi] for hi in range(2)]


def adam(factor, kept, far, own, one, two):
    grad = (kept + far.astype(F32)) * factor
    one = beta_first * one + (1.0 - beta_first) * grad
    two = beta_second * two + (1.0 - beta_second) * grad * grad
    wide = own.astype(F32)
    updated = wide - inner_rate * (one / (jnp.sqrt(two) + adam_eps) + decay_rate * wide)
    return one, two, updated


def outer_update(mean_drift, global_weights, outer_moment):
    mean_drift = mean_drift.astype(F32)
    new_moment = outer_beta * outer_moment + mean_drift
    return global_weights - outer_rate * (mean_drift + outer_beta * new_moment)


def outer_kernel(pieces, global_weights, outer_moment, out):
    share, rows = pieces.shape[0], pieces.shape[1]
    for i in range(share):
        at = slice(i * rows, (i + 1) * rows)
        out[at] = outer_update(pieces[i], global_weights[at], outer_moment[at])


def first_update_kernel(
    factor, kept, far, own, one, two, pieces, global_weights, outer_moment, new, new_one, new_two
):
    share, rows = pieces.shape[0], pieces.shape[1]
    for i in range(share):
        at = slice(i * rows, (i + 1) * rows)
        first, second, updated = adam(factor, kept[at], far[at], own[at], one[at], two[at])
        outer = outer_update(pieces[i], global_weights[at], outer_moment[at])
        new_one[at] = first
        new_two[at] = second
        new[at] = (mix_share * updated + (1.0 - mix_share) * outer).astype(BF)


def update_kernel(factor, kept, far, own, one, two, *rest):
    done, out = rest[:-1], rest[-1]
    _, _, updated = adam(factor, kept[...], far[...], own[...], one[...], two[...])
    cols = updated.shape[1]
    if done:
        for k, block in enumerate(done):
            out[0, :, k * cols : (k + 1) * cols] = block[...]
        out[0, :, len(done) * cols :] = updated.astype(BF)
    else:
        out[...] = updated.astype(BF)


def per_device(
    inputs, targets, weights, first_moment, second_moment, global_weights, outer_moment, drift
):
    place = lax.axis_index("fsdp").astype(jnp.int32).reshape(1)
    tok_rows, width = inputs.shape[2], inputs.shape[3]
    tokens_total = tok_rows * lax.axis_size("fsdp")
    scale = width ** (-0.5)
    rows, columns = weights.shape[1], weights.shape[2]
    wide = columns // CHUNKS
    cols = wide // 2
    factor = scale / tokens_total
    replicas = lax.axis_size("rep")
    groups = planes(replicas)
    share = len(groups[0])

    def prepare(step, wanted, gates):
        return call(
            functools.partial(prepare_kernel, step, wanted, rows),
            [shaped((tok_rows, 2 * rows), BF)] * len(wanted),
            [place, inputs],
            gates,
            [SCALAR, ANY],
            limit=PREPARE_LIMIT,
            scratch=[pltpu.SemaphoreType.DMA((2 * len(wanted),))],
        )

    def chunk(lead, k):
        at = lead + (0, k)
        height = tok_rows if len(lead) > 1 else rows
        return pl.BlockSpec((None,) * len(lead) + (height, wide), lambda i: at)

    def keys(step, groups, feats, chunks, own, far, gates):
        views, specs = [], []
        for k in chunks:
            views += [targets, own, far]
            specs += [chunk((step, 0), k)] + ([chunk((0,), k)] if step == 0 else [FULL]) * 2
        count = len(groups)
        return call(
            functools.partial(keys_kernel, scale, count, groups[0] == 0),
            [shaped((count * tok_rows, len(chunks) * cols), F32)] * 2,
            [place, *[feats[g] for g in groups], *views],
            gates,
            [SCALAR] + [FULL] * count + specs,
            scratch=[pltpu.VMEM((tok_rows, wide), F32)],
        )

    def turn(feats, gates):
        return call(turn_kernel, [shaped((rows, 4 * tok_rows), BF)] * 2, feats, gates)

    def core_sum(pairs, gates):
        blocks = []
        for kept, sent in pairs:
            blocks += [kept, pair_swap(sent, 1)]
        height = pairs[0][0].shape[0]
        return call(
            functools.partial(core_sum_kernel, tok_rows),
            shaped((height, columns // 2), BF),
            blocks,
            gates,
        )

    def residuals(ours, theirs, gates):
        out = shaped((4 * tok_rows, columns // 2), BF)
        return call(residual_kernel, out, [*ours, *theirs], gates)

    def grads(dtype, parts, feats, mine, other, gates):
        return call(
            grads_kernel,
            [shaped((rows, columns // parts), dtype)] * parts,
            [place, feats, mine, other],
            gates,
            [SCALAR] + [FULL] * 3,
            scratch=[pltpu.VMEM((4 * tok_rows, columns), BF)],
        )

    def first_update(k, kept, far, gates):
        state = chunk((0,), k)
        outer = chunk((), k)
        block = shaped((rows, wide), F32)
        pieces = pl.BlockSpec((share, rows_of, wide), lambda i: (0, 0, k))
        return call(
            functools.partial(first_update_kernel, factor),
            [shaped((rows, wide), BF), block, block],
            [kept, far, weights, first_moment, second_moment, means, global_weights, outer_moment],
            gates,
            [outer, FULL, state, state, state, pieces, outer, outer],
        )

    def update(k, kept, far, own, one, two, done, gates):
        return call(
            functools.partial(update_kernel, factor),
            shaped((1, rows, columns) if done else (rows, wide), BF),
            [kept, far, own, one, two, *done],
            gates,
            [chunk((), k)] + [FULL] * (4 + len(done)),
        )

    far = far_swap(weights)
    packs = prepare(0, (0, 1, 2, 3), [])
    feats = [packs[0]] + [pair_swap(packs[g], g) for g in (1, 2, 3)]
    rows_of = rows // share
    casted = call(cast_kernel, shaped((share, rows_of, columns), BF), [drift], [feats[1]])
    pieces = lax.all_to_all(casted, "rep", 0, 0, axis_index_groups=groups)
    (keep,) = prepare(1, (0,), [casted])
    summed = call(sum_kernel, shaped((rows_of, columns), BF), [pieces], [keep])
    summed_other = swap(summed, "rep", lambda i: i ^ 4)

    near_keys = keys(0, (0, 1), feats, (0, 1), weights, far, [summed])
    pair_keys = keys(0, (2, 3), feats, (0, 1), weights, far, [near_keys[0]])
    near_part = core_sum([near_keys], [])
    near_other = pair_swap(near_part, 2)
    pair_part = core_sum([pair_keys], [near_part])
    pair_other = pair_swap(pair_part, 2)
    own_t, far_t = turn(feats, [pair_part, summed_other, near_other])
    mine = residuals([near_part, pair_part], [near_other, pair_other], [far_t])
    other = pair_swap(mine, 1)
    across_a, across_b = grads(BF, CHUNKS, far_t, mine, other, [])
    far_a, far_b = far_swap(across_a), far_swap(across_b)
    (kept,) = grads(F32, 1, own_t, mine, other, [across_b])
    copies = call(
        functools.partial(mean_kernel, replicas),
        shaped((share, rows_of, columns), BF),
        [summed, summed_other],
        [kept],
    )
    means = lax.all_to_all(copies, "rep", 0, 0, axis_index_groups=groups)
    packs = prepare(1, (1, 2, 3), [copies])
    later = [keep] + [pair_swap(packs[g - 1], g) for g in (1, 2, 3)]
    own_a, one_a, two_a = first_update(0, kept, far_a, [packs[0]])
    gather_a = far_swap(own_a)
    own_b, one_b, two_b = first_update(1, kept, far_b, [own_a, *later[1:3]])
    gather_b = far_swap(own_b)

    every = (0, 1, 2, 3)
    keys_a = keys(1, every, later, (0,), own_a, gather_a, [own_b])
    keys_b = keys(1, every, later, (1,), own_b, gather_b, [keys_a[0]])
    part = core_sum([keys_a, keys_b], [])
    own_t, far_t = turn(later, [part])
    mine = residuals([part], [pair_swap(part, 2)], [far_t])
    other = pair_swap(mine, 1)
    across_a, across_b = grads(BF, CHUNKS, far_t, mine, other, [])
    far_a, far_b = far_swap(across_a), far_swap(across_b)
    (kept,) = grads(F32, 1, own_t, mine, other, [across_b])
    global_out = call(
        outer_kernel,
        shaped((rows, columns), F32),
        [means, global_weights, outer_moment],
        [kept],
    )
    done_a = update(0, kept, far_a, own_a, one_a, two_a, [], [])
    weights_out = update(1, kept, far_b, own_b, one_b, two_b, [done_a], [])
    return (weights_out, global_out)


def solution(mesh):
    in_specs = (
        P(None, "rep", "fsdp", None),
        P(None, "rep", "fsdp", None),
        P("rep", "fsdp", None),
        P("rep", "fsdp", None),
        P("rep", "fsdp", None),
        P("fsdp", None),
        P("fsdp", None),
        P("rep", "fsdp", None),
    )
    out_specs = (P("rep", "fsdp", None), P("fsdp", None))
    return jax.shard_map(
        per_device, mesh=mesh, in_specs=in_specs, out_specs=out_specs, check_vma=False
    )
```

```python
import functools

import jax
import jax.numpy as jnp
from jax import lax
from jax.experimental import pallas as pl
from jax.experimental.pallas import tpu as pltpu
from jax.sharding import PartitionSpec as P

CHUNKS = 2

inner_rate = 0.2
beta_first = 0.9
beta_second = 0.95
adam_eps = 1e-08
decay_rate = 0.1
mix_share = 0.5
outer_rate = 0.7
outer_beta = 0.9

BF = jnp.bfloat16
F32 = jnp.float32
VMEM_LIMIT = 16 << 20
PREPARE_LIMIT = 56 << 20
FLOPS = 10**11

ANY = pl.BlockSpec(memory_space=pl.ANY)
FULL = pl.BlockSpec(memory_space=pltpu.VMEM)
SCALAR = pl.BlockSpec(memory_space=pltpu.SMEM)


def swap(value, axis, change):
    pairs = [(i, change(i)) for i in range(lax.axis_size(axis))]
    return lax.ppermute(value, axis, pairs)


def pair_swap(value, g):
    return swap(value, "fsdp", lambda i: i ^ g)


def far_swap(value):
    return swap(value, "fsdp", lambda i: i ^ 6)


def shaped(shape, dtype):
    return jax.ShapeDtypeStruct(shape, dtype)


def call(body, outs, operands, gates=(), specs=None, limit=VMEM_LIMIT, scratch=(), out_specs=None, aliases={}):
    n = len(gates)
    size = sum(v.size * v.dtype.itemsize for v in operands)

    def kernel(*refs):
        body(*refs[n:])

    return pl.pallas_call(
        kernel,
        name=getattr(body, "func", body).__name__.removesuffix("_kernel"),
        grid=(1,),
        out_shape=outs,
        in_specs=[ANY] * n + (specs or [FULL] * len(operands)),
        out_specs=out_specs or jax.tree.map(lambda _: FULL, outs),
        input_output_aliases=aliases,
        scratch_shapes=scratch,
        compiler_params=pltpu.CompilerParams(vmem_limit_bytes=limit),
        cost_estimate=pl.CostEstimate(flops=FLOPS, bytes_accessed=size, transcendentals=0),
    )(*gates, *operands)


def prepare_kernel(step, groups, depth, place, feats, *refs):
    outs, done = refs[:-1], refs[-1]
    copies = []
    for g, out in zip(groups, outs):
        at = place[0] ^ g
        for j, shard in enumerate((at, at ^ 6)):
            columns = pl.ds(pl.multiple_of(shard * depth, depth), depth)
            copies.append(
                pltpu.make_async_copy(
                    feats.at[step, 0, :, columns],
                    out.at[:, j * depth : (j + 1) * depth],
                    done.at[len(copies)],
                )
            )
    for copy in copies:
        copy.start()
    for copy in copies:
        copy.wait()


def keys_kernel(scale, count, own_first, place, *refs):
    feats, chunks, (kept, sent, whole) = refs[:count], refs[count:-3], refs[-3:]
    rows = feats[0].shape[0]
    core = place[0] % 2
    for k in range(len(chunks) // 3):
        aims, own, far = chunks[3 * k : 3 * k + 3]
        depth, cols = own.shape[0], own.shape[1] // 2
        for g in range(count):
            part = jnp.dot(feats[g][:, :depth], own[...], preferred_element_type=F32)
            part += jnp.dot(feats[g][:, depth:], far[...], preferred_element_type=F32)
            part *= scale
            if g == 0 and own_first:
                part -= aims[...].astype(F32)
            whole[...] = part
            for half, out in ((1 - core, sent), (core, kept)):
                columns = pl.ds(pl.multiple_of(half * cols, cols), cols)
                out[g * rows : (g + 1) * rows, k * cols : (k + 1) * cols] = whole[
                    :, columns
                ].astype(out.dtype)


def core_sum_kernel(rows, *refs):
    pairs, out = refs[:-1], refs[-1]
    cols = pairs[0].shape[1]
    for k in range(len(pairs) // 2):
        kept, other = pairs[2 * k : 2 * k + 2]
        for g in range(out.shape[0] // rows):
            here, there = g * rows, (g ^ 1) * rows
            total = kept[here : here + rows] + other[there : there + rows].astype(F32)
            out[here : here + rows, k * cols : (k + 1) * cols] = total.astype(BF)


def turn_kernel(*refs):
    feats, outs = refs[:4], refs[4:]
    rows, depth = feats[0].shape[0], outs[0].shape[0]
    for j, out in enumerate(outs):
        for g in range(4):
            out[:, g * rows : (g + 1) * rows] = feats[g][:, j * depth : (j + 1) * depth].T


def residual_kernel(*refs):
    ours, theirs, out = refs[: len(refs) // 2], refs[len(refs) // 2 : -1], refs[-1]
    half = out.shape[0] // 2
    if len(ours) == 1:
        ours = (ours[0].at[:half], ours[0].at[half:])
        theirs = (theirs[0].at[:half], theirs[0].at[half:])
    for i in range(2):
        total = ours[i][...].astype(F32) + theirs[1 - i][...].astype(F32)
        out[i * half : (i + 1) * half] = total.astype(BF)


def grads_kernel(place, feats, mine, other, *refs):
    outs, whole = refs[:-1], refs[-1]
    rows = mine.shape[0] // 4
    core = place[0] % 2
    cols = mine.shape[1] // CHUNKS
    for k in range(CHUNKS):
        part = slice(k * cols, (k + 1) * cols)
        for half, residual, flip in ((core, mine, 0), (1 - core, other, 1)):
            columns = pl.ds(pl.multiple_of((2 * k + half) * cols, cols), cols)
            for g in range(4):
                there = (g ^ flip) * rows
                whole[g * rows : (g + 1) * rows, columns] = residual[there : there + rows, part]
    cols = outs[0].shape[1]
    for k, out in enumerate(outs):
        part = whole[:, k * cols : (k + 1) * cols]
        grad = jnp.dot(feats[...], part, preferred_element_type=F32)
        out[...] = grad.astype(out.dtype)


def cast_kernel(drift, out):
    share, rows = out.shape[0], out.shape[1]
    for i in range(share):
        out[i] = drift[0, i * rows : (i + 1) * rows].astype(BF)


def sum_kernel(pieces, out):
    out[...] = jnp.sum(pieces[...].astype(F32), axis=0).astype(BF)


def mean_kernel(replicas, part, other, out):
    mean = ((part[...].astype(F32) + other[...].astype(F32)) / replicas).astype(BF)
    out[...] = jnp.broadcast_to(mean[None], out.shape)


def planes(size):
    return [[i for i in range(size) if (i // 4) % 2 == hi] for hi in range(2)]


def adam(factor, kept, far, own, one, two):
    grad = (kept + far.astype(F32)) * factor
    one = beta_first * one + (1.0 - beta_first) * grad
    two = beta_second * two + (1.0 - beta_second) * grad * grad
    wide = own.astype(F32)
    updated = wide - inner_rate * (one / (jnp.sqrt(two) + adam_eps) + decay_rate * wide)
    return one, two, updated


def outer_update(mean_drift, global_weights, outer_moment):
    mean_drift = mean_drift.astype(F32)
    new_moment = outer_beta * outer_moment + mean_drift
    return global_weights - outer_rate * (mean_drift + outer_beta * new_moment)


def outer_kernel(pieces, global_weights, outer_moment, out):
    share, rows = pieces.shape[0], pieces.shape[1]
    for i in range(share):
        at = slice(i * rows, (i + 1) * rows)
        out[at] = outer_update(pieces[i], global_weights[at], outer_moment[at])


def first_update_kernel(
    factor, kept, far, own, one, two, pieces, global_weights, outer_moment, new, new_one, new_two
):
    share, rows = pieces.shape[0], pieces.shape[1]
    for i in range(share):
        at = slice(i * rows, (i + 1) * rows)
        first, second, updated = adam(factor, kept[at], far[at], own[at], one[at], two[at])
        outer = outer_update(pieces[i], global_weights[at], outer_moment[at])
        new_one[at] = first
        new_two[at] = second
        new[at] = (mix_share * updated + (1.0 - mix_share) * outer).astype(BF)


def update_kernel(factor, kept, far, own, one, two, *rest):
    _, _, updated = adam(factor, kept[...], far[...], own[...], one[...], two[...])
    rest[-1][...] = updated.astype(BF)


def per_device(
    inputs, targets, weights, first_moment, second_moment, global_weights, outer_moment, drift
):
    place = lax.axis_index("fsdp").astype(jnp.int32).reshape(1)
    tok_rows, width = inputs.shape[2], inputs.shape[3]
    tokens_total = tok_rows * lax.axis_size("fsdp")
    scale = width ** (-0.5)
    rows, columns = weights.shape[1], weights.shape[2]
    wide = columns // CHUNKS
    cols = wide // 2
    factor = scale / tokens_total
    replicas = lax.axis_size("rep")
    groups = planes(replicas)
    share = len(groups[0])

    def prepare(step, wanted, gates):
        return call(
            functools.partial(prepare_kernel, step, wanted, rows),
            [shaped((tok_rows, 2 * rows), BF)] * len(wanted),
            [place, inputs],
            gates,
            [SCALAR, ANY],
            limit=PREPARE_LIMIT,
            scratch=[pltpu.SemaphoreType.DMA((2 * len(wanted),))],
        )

    def chunk(lead, k):
        at = lead + (0, k)
        height = tok_rows if len(lead) > 1 else rows
        return pl.BlockSpec((None,) * len(lead) + (height, wide), lambda i: at)

    def keys(step, groups, feats, chunks, own, far, gates):
        views, specs = [], []
        for k in chunks:
            views += [targets, own, far]
            specs += [chunk((step, 0), k)] + ([chunk((0,), k)] if step == 0 else [FULL]) * 2
        count = len(groups)
        return call(
            functools.partial(keys_kernel, scale, count, groups[0] == 0),
            [shaped((count * tok_rows, len(chunks) * cols), kind) for kind in (F32, BF)],
            [place, *[feats[g] for g in groups], *views],
            gates,
            [SCALAR] + [FULL] * count + specs,
            scratch=[pltpu.VMEM((tok_rows, wide), F32)],
        )

    def turn(feats, gates):
        return call(turn_kernel, [shaped((rows, 4 * tok_rows), BF)] * 2, feats, gates)

    def core_sum(pairs, gates):
        blocks = []
        for kept, sent in pairs:
            blocks += [kept, pair_swap(sent, 1)]
        height = pairs[0][0].shape[0]
        return call(
            functools.partial(core_sum_kernel, tok_rows),
            shaped((height, columns // 2), BF),
            blocks,
            gates,
        )

    def residuals(ours, theirs, gates):
        out = shaped((4 * tok_rows, columns // 2), BF)
        return call(residual_kernel, out, [*ours, *theirs], gates)

    def grads(dtype, parts, feats, mine, other, gates):
        return call(
            grads_kernel,
            [shaped((rows, columns // parts), dtype)] * parts,
            [place, feats, mine, other],
            gates,
            [SCALAR] + [FULL] * 3,
            scratch=[pltpu.VMEM((4 * tok_rows, columns), BF)],
        )

    def first_update(k, kept, far, gates):
        state = chunk((0,), k)
        outer = chunk((), k)
        block = shaped((rows, wide), F32)
        pieces = pl.BlockSpec((share, rows_of, wide), lambda i: (0, 0, k))
        return call(
            functools.partial(first_update_kernel, factor),
            [shaped((rows, wide), BF), block, block],
            [kept, far, weights, first_moment, second_moment, means, global_weights, outer_moment],
            gates,
            [outer, FULL, state, state, state, pieces, outer, outer],
        )

    def update(k, kept, far, own, one, two, done, gates):
        return call(
            functools.partial(update_kernel, factor),
            shaped((1, rows, columns), BF),
            [kept, far, own, one, two, *done],
            gates,
            [chunk((), k)] + [FULL] * 4 + [ANY] * len(done),
            out_specs=chunk((0,), k),
            aliases={len(gates) + 5: 0} if done else {},
        )

    far = far_swap(weights)
    packs = prepare(0, (0, 1, 2, 3), [])
    feats = [packs[0]] + [pair_swap(packs[g], g) for g in (1, 2, 3)]
    rows_of = rows // share
    casted = call(cast_kernel, shaped((share, rows_of, columns), BF), [drift], [feats[1]])
    pieces = lax.all_to_all(casted, "rep", 0, 0, axis_index_groups=groups)
    (keep,) = prepare(1, (0,), [casted])
    summed = call(sum_kernel, shaped((rows_of, columns), BF), [pieces], [keep])
    summed_other = swap(summed, "rep", lambda i: i ^ 4)

    near_keys = keys(0, (0, 1), feats, (0, 1), weights, far, [summed])
    pair_keys = keys(0, (2, 3), feats, (0, 1), weights, far, [near_keys[0]])
    near_part = core_sum([near_keys], [])
    near_other = pair_swap(near_part, 2)
    pair_part = core_sum([pair_keys], [near_part])
    pair_other = pair_swap(pair_part, 2)
    own_t, far_t = turn(feats, [pair_part, summed_other, near_other])
    mine = residuals([near_part, pair_part], [near_other, pair_other], [far_t])
    other = pair_swap(mine, 1)
    across_a, across_b = grads(BF, CHUNKS, far_t, mine, other, [])
    far_a, far_b = far_swap(across_a), far_swap(across_b)
    (kept,) = grads(F32, 1, own_t, mine, other, [across_b])
    copies = call(
        functools.partial(mean_kernel, replicas),
        shaped((share, rows_of, columns), BF),
        [summed, summed_other],
        [kept],
    )
    means = lax.all_to_all(copies, "rep", 0, 0, axis_index_groups=groups)
    packs = prepare(1, (1, 2, 3), [copies])
    later = [keep] + [pair_swap(packs[g - 1], g) for g in (1, 2, 3)]
    own_a, one_a, two_a = first_update(0, kept, far_a, [packs[0]])
    gather_a = far_swap(own_a)
    own_b, one_b, two_b = first_update(1, kept, far_b, [own_a, *later[1:3]])
    gather_b = far_swap(own_b)

    every = (0, 1, 2, 3)
    keys_a = keys(1, every, later, (0,), own_a, gather_a, [own_b])
    keys_b = keys(1, every, later, (1,), own_b, gather_b, [keys_a[0]])
    part = core_sum([keys_a, keys_b], [])
    own_t, far_t = turn(later, [part])
    mine = residuals([part], [pair_swap(part, 2)], [far_t])
    other = pair_swap(mine, 1)
    across_a, across_b = grads(BF, CHUNKS, far_t, mine, other, [])
    far_a, far_b = far_swap(across_a), far_swap(across_b)
    (kept,) = grads(F32, 1, own_t, mine, other, [across_b])
    global_out = call(
        outer_kernel,
        shaped((rows, columns), F32),
        [means, global_weights, outer_moment],
        [kept],
    )
    done_a = update(0, kept, far_a, own_a, one_a, two_a, [], [])
    weights_out = update(1, kept, far_b, own_b, one_b, two_b, [done_a], [])
    return (weights_out, global_out)


def solution(mesh):
    in_specs = (
        P(None, "rep", "fsdp", None),
        P(None, "rep", "fsdp", None),
        P("rep", "fsdp", None),
        P("rep", "fsdp", None),
        P("rep", "fsdp", None),
        P("fsdp", None),
        P("fsdp", None),
        P("rep", "fsdp", None),
    )
    out_specs = (P("rep", "fsdp", None), P("fsdp", None))
    return jax.shard_map(
        per_device, mesh=mesh, in_specs=in_specs, out_specs=out_specs, check_vma=False
    )
```
